256 devices in a mesh: row: 16 (over z_hi, x), col: 16 (over y, z_lo, core).
Axes of the slice: x: 4, y: 4, z: 8 (z_hi: 4, z_lo: 2; z = z_hi * 2 + z_lo), core: 2. Of those that a mesh axis runs over, the one named last changes fastest.
Arguments:
- inputs: bfloat16 [2048, 16384], P('col', 'row'), may hold values from -0.13183594 to 0.13183594
- weight: bfloat16 [16384, 26624], P('row', 'col'), may hold values from -0.046875 to 0.046875
- grad_out: bfloat16 [2048, 26624], P('row', 'col'), may hold values from -6 to 6
Outputs:
- grad_inputs: bfloat16 [2048, 16384], P('col', 'row')
- grad_weight: bfloat16 [16384, 26624], P('row', 'col')
The draws below stay inside these ranges and needn't reach their ends.
All inputs are finite; a program needn't handle non-finite values.
Results may differ from the reference program's by a relative error of at most 0.001.
Values may be sent and summed in bfloat16 or wider, within the bound.
A program may use at most 128 MiB of HBM per device.

```python
import jax
import jax.numpy as jnp
from jax import lax

D = 16384
FF = 26624
TOKENS = 2048


def spiked(entries, rng, source, target, shards_of, factor):
    def block_of(dim):
        return (jnp.arange(entries.shape[dim]) // (entries.shape[dim] // shards_of)).reshape((-1,) + (1,) * (entries.ndim - 1 - dim))

    first = jax.random.permutation(rng, shards_of)[block_of(target)]
    second = (block_of(target) + shards_of // 2) % shards_of
    return jnp.where((block_of(source) == first) | (block_of(source) == second), factor * entries, entries)


def levels(own_key, shape, split, low, high):
    loudness = 1.0
    for position, parts in split:
        heights = jax.random.uniform(jax.random.fold_in(jax.random.fold_in(own_key, 6), position), (parts,), jnp.float32, low / len(split), high / len(split))
        loudness = loudness * jnp.repeat(jnp.exp(heights), shape[position] // parts).reshape((-1,) + (1,) * (len(shape) - 1 - position))
    return loudness


def bell_draw(key, dims, width, reach, shards=(), held_as=jnp.bfloat16):
    values = jax.random.normal(key, dims, jnp.float32) * width
    if len(shards) > 0:
        values = levels(key, dims, shards, -0.22, 0.18) * values
    return jnp.clip(values, min=-reach, max=reach).astype(held_as)


def bell_draw_with(own_key, dims, deviation, reach, shards, heavy, kind=jnp.bfloat16):
    entries = deviation * jax.random.normal(own_key, dims, jnp.float32)
    if shards:
        entries = entries * levels(own_key, dims, shards, -0.22, 0.18)
    return jnp.clip(spiked(entries, jax.random.fold_in(own_key, 3), *heavy), -reach, reach).astype(kind)


def setup_inputs(seed: int = 0) -> dict:
    keys = jax.random.split(jax.random.key(seed), 4)
    inputs = bell_draw(keys[0], (TOKENS, D), (TOKENS ** -0.5), 0.13183594, ((0, 16), (1, 16)))
    weight = bell_draw(keys[1], (D, FF), D ** -0.5, 0.046875, ((0, 16), (1, 16)))
    grad_out = bell_draw_with(keys[2], (TOKENS, FF), 1.0, 6.0, ((0, 16), (1, 16)), (1, 0, 16, 2.0))
    return {"inputs": inputs, "weight": weight, "grad_out": grad_out}


def reference(inputs, weight, grad_out):
    grad_inputs = lax.dot_general(grad_out, weight, (((1,), (1,)), ((), ())), preferred_element_type=jnp.float32)
    grad_weight = lax.dot_general(inputs, grad_out, (((0,), (0,)), ((), ())), preferred_element_type=jnp.float32)
    return grad_inputs.astype(jnp.bfloat16), grad_weight.astype(jnp.bfloat16)
```

```python
import functools

import jax
import jax.numpy as jnp
from jax import lax
from jax.experimental import pallas as pl
from jax.experimental.pallas import tpu as pltpu
from jax.sharding import PartitionSpec as P

MESH = pl.DeviceIdType.MESH

SLOTS = [
    (0, 0), (0, 1), (0, 3), (0, 2), (1, 0), (3, 0), (1, 1), (1, 3),
    (3, 1), (3, 3), (2, 0), (1, 2), (2, 1), (2, 3), (3, 2), (2, 2),
]
SLOT = {ij: s for s, ij in enumerate(SLOTS)}
EVEN = [s for s, (_, j) in enumerate(SLOTS) if j % 2 == 0]
ODD = [s for s, (_, j) in enumerate(SLOTS) if j % 2 == 1]
RANK = [EVEN.index(s) if s in EVEN else ODD.index(s) for s in range(16)]
LAG = 2


def table(index, values):
    out = jnp.int32(values[0])
    for at, value in enumerate(values[1:], 1):
        out = jnp.where(index == at, jnp.int32(value), out)
    return out


def kernel(
    in_ref, w_ref, go_ref, gin_ref, gw_ref,
    go, tin, w, acc, part, dbuf, ybuf, zbuf, stage, raw, gout,
    zs, zr, xs, xr, tys, tyr, tzs, tzr, tcs, tcr, ds, dr, ys, yr, rs, rr, ls, os,
):
    row, col = lax.axis_index("row"), lax.axis_index("col")
    zh, x = row // 4, lax.rem(row, 4)
    y, zl, core = col // 4, lax.rem(col // 2, 2), lax.rem(col, 2)
    tokens = raw.shape[0]
    half = tokens // 2
    width = tin.shape[1]

    def wrap(v):
        return lax.rem(v + 4, 4)

    def x_peer(d):
        return (zh * 4 + wrap(x + d), col)

    def z_peer(d):
        return (wrap(zh + d) * 4 + x, col)

    def kcol(yy, q, c):
        return (wrap(yy) * 2 + lax.rem(zl + q, 2)) * 2 + c

    def y_peer(d):
        return (row, kcol(y + d, 0, core))

    zl_peer = (row, kcol(y, 1, core))
    core_peer = (row, kcol(y, 0, 1 - core))

    def remote(src, dst, send, recv, to):
        return pltpu.make_async_remote_copy(
            src_ref=src, dst_ref=dst, send_sem=send, recv_sem=recv, device_id=to, device_id_type=MESH
        )

    def rows_of(slot, h):
        return pl.ds(slot * tokens + h * half, half)

    def z_copy(d, c):
        sign = 1 - 2 * d
        back = 3 if d == 0 else 1
        h = d if c != 1 else 1 - d
        src, dst = (SLOT[back, 0], SLOT[2, 0]) if c == 2 else (SLOT[0, 0], SLOT[back, 0])
        return remote(go.at[rows_of(src, h)], go.at[rows_of(dst, h)], zs.at[d, c], zr.at[d, c], z_peer(sign))

    def x_copy(i, d, c):
        sign = 1 - 2 * d
        back = 3 if d == 0 else 1
        h = d if c != 1 else 1 - d
        src, dst = (SLOT[i, back], SLOT[i, 2]) if c == 2 else (SLOT[i, 0], SLOT[i, back])
        return remote(go.at[rows_of(src, h)], go.at[rows_of(dst, h)], xs.at[i, d, c], xr.at[i, d, c], x_peer(sign))

    def t_copy(q, d, c):
        sign = 1 - 2 * d
        h = d if c != 1 else 1 - d
        k = kcol(y - sign, q, core) if c == 2 else kcol(y, q, core)
        part_of = tin.at[k, pl.ds(h * (width // 2), width // 2)]
        return remote(part_of, part_of, tys.at[q, d, c], tyr.at[q, d, c], y_peer(sign))

    def t_zl():
        block = tin.at[kcol(y, 0, core)]
        return remote(block, block, tzs, tzr, zl_peer)

    def t_core(q, e):
        if e < 3:
            block = tin.at[kcol(y + (0, 1, 3)[e], q, core)]
        else:
            block = tin.at[kcol(y + 2, q, core), pl.ds((e - 3) * (width // 2), width // 2)]
        return remote(block, block, tcs.at[q, e], tcr.at[q, e], core_peer)

    loads = [
        pltpu.make_async_copy(go_ref, go.at[pl.ds(0, tokens)], ls.at[0]),
        pltpu.make_async_copy(in_ref, raw, ls.at[1]),
        pltpu.make_async_copy(w_ref, w, ls.at[2]),
    ]
    for load in loads:
        load.start()

    barrier = pltpu.get_barrier_semaphore()
    for to in (x_peer(1), x_peer(3), z_peer(1), z_peer(3), y_peer(1), y_peer(3), zl_peer, core_peer):
        pl.semaphore_signal(barrier, inc=1, device_id=to, device_id_type=MESH)
    pl.semaphore_wait(barrier, 8)

    loads[0].wait()
    for c in range(2):
        for d in range(2):
            z_copy(d, c).start()
            x_copy(0, d, c).start()
    loads[1].wait()
    tin[kcol(y, 0, core)] = raw[...].T
    for c in range(2):
        for d in range(2):
            t_copy(0, d, c).start()
    t_core(0, 0).start()
    acc[...] = jnp.zeros_like(acc)
    loads[2].wait()

    def x_recv(i, c):
        for d in range(2):
            x_copy(i, d, c).wait_recv()

    def x_send(i, c):
        for d in range(2):
            x_copy(i, d, c).start()

    def t_far(q):
        for d in range(2):
            t_copy(q, d, 0).wait_recv()
        for d in range(2):
            t_copy(q, d, 2).start()
        for d in range(2):
            t_copy(q, d, 1).wait_recv()
            t_core(q, 2 - d).start()

    def t_far_core(q):
        for d in range(2):
            t_copy(q, d, 2).wait_recv()
            t_core(q, 3 + d).start()

    def before_1():
        x_recv(0, 0)
        x_send(0, 2)
        t_far(0)
        x_recv(0, 1)

    def before_3():
        for d in range(2):
            z_copy(d, 0).wait_recv()
        for d in range(2):
            z_copy(d, 2).start()
        x_copy(1, 0, 1).start()
        x_copy(1, 1, 0).start()
        x_copy(3, 0, 0).start()
        x_copy(3, 1, 1).start()
        t_zl().start()
        t_far_core(0)
        x_recv(0, 2)

    def before_4():
        for d in range(2):
            z_copy(d, 1).wait_recv()
        x_copy(1, 0, 0).start()
        x_copy(1, 1, 1).start()
        x_copy(3, 0, 1).start()
        x_copy(3, 1, 0).start()

    def before_6():
        x_recv(1, 0)
        x_recv(1, 1)
        x_send(1, 2)

    def before_8():
        for d in range(2):
            z_copy(d, 2).wait_recv()
        for c in range(2):
            x_send(2, c)
        x_recv(3, 0)
        x_recv(3, 1)
        x_send(3, 2)

    def before_10():
        t_zl().wait_recv()
        for c in range(2):
            for d in range(2):
                t_copy(1, d, c).start()
        t_core(1, 0).start()

    def before_11():
        x_recv(1, 2)

    def before_12():
        x_recv(2, 0)
        x_send(2, 2)
        t_far(1)
        x_recv(2, 1)

    def before_13():
        t_far_core(1)
        for q in range(2):
            for e in range(5):
                t_core(q, e).wait_recv()

    def before_14():
        x_recv(3, 2)

    def before_15():
        x_recv(2, 2)

    before = {
        1: before_1, 3: before_3, 4: before_4, 6: before_6, 8: before_8, 10: before_10,
        11: before_11, 12: before_12, 13: before_13, 14: before_14, 15: before_15,
    }

    def place(s):
        i, j = table(s, [i for i, _ in SLOTS]), table(s, [j for _, j in SLOTS])
        own = core == lax.rem(x + j, 2)
        return table(s, RANK), own, lax.rem(zh + i - y + 8, 4), wrap(x + j) // 2

    def d_copy(s, n):
        return remote(part.at[s], dbuf.at[n], ds.at[n], dr.at[n], core_peer)

    def y_copy(s, n, d, h):
        return remote(part.at[s, h], ybuf.at[n, d, h], ys.at[n, h], yr.at[n, d, h], y_peer(1 - 2 * d))

    def r_copy(s):
        return remote(part.at[s], zbuf, rs, rr, zl_peer)

    def share(s):
        block = go[pl.ds(pl.multiple_of(s * tokens, tokens), tokens), :]
        for h in range(2):
            part[s, h] = lax.dot_general(
                block, w[pl.ds(h * (width // 2), width // 2), :], (((1,), (1,)), ((), ())),
                preferred_element_type=jnp.float32,
            )

    def sum_cores(s):
        n, own, ahead, _ = place(s)

        @pl.when(own)
        def _():
            d_copy(s, n).wait_recv()
            part[s] += dbuf[n]

            @pl.when(ahead == 2)
            def _():
                y_copy(s, n, 0, 0).start()
                y_copy(s, n, 1, 1).start()

            @pl.when(ahead == 1)
            def _():
                y_copy(s, n, 0, 1).start()

            @pl.when(ahead == 3)
            def _():
                y_copy(s, n, 1, 0).start()

    def sum_far(s):
        n, own, ahead, _ = place(s)
        for d in range(2):

            @pl.when(jnp.logical_and(own, ahead == 1 + 2 * d))
            def _():
                y_copy(s, n, d, d).wait_recv()
                part[s, d] += ybuf[n, d, d]
                y_copy(s, n, d, d).start()

    def sum_near(s):
        n, own, ahead, z_to = place(s)

        @pl.when(jnp.logical_and(own, ahead == 0))
        def _():
            for d in range(2):
                for h in range(2):
                    y_copy(s, n, d, h).wait_recv()
            part[s] += ybuf[n, 0] + ybuf[n, 1]

            @pl.when(z_to != zl)
            def _():
                r_copy(s).start()

    tile = width // 4

    def out_copy(r):
        at = pl.ds(pl.multiple_of(r * tile, tile), tile)
        return pltpu.make_async_copy(stage.at[at], gw_ref.at[at], os.at[r])

    def weights(g):
        ks = []
        for e in range(4):
            i, j = (table(g, [SLOTS[4 * gg + e][axis] for gg in range(4)]) for axis in range(2))
            ks.append(wrap(zh + i) * 4 + wrap(x + j))

        def rows_tile(r, carry):
            at = pl.ds(pl.multiple_of(r * tile, tile), tile)
            left = jnp.concatenate([tin[k, at, :] for k in ks], axis=1)
            right = go[pl.ds(pl.multiple_of(g * 4 * tokens, 4 * tokens), 4 * tokens), :]
            acc[at, :] += lax.dot_general(
                left, right, (((1,), (0,)), ((), ())), preferred_element_type=jnp.float32
            )

            @pl.when(g == 3)
            def _():
                stage[at, :] = acc[at, :].astype(stage.dtype)
                out_copy(r).start()

            return carry

        lax.fori_loop(0, 4, rows_tile, 0)

    def step(s, carry):
        for at, event in before.items():
            pl.when(s == at)(event)

        @pl.when(s < 16)
        def _():
            share(s)
            n, own, _, _ = place(s)

            @pl.when(jnp.logical_not(own))
            def _():
                d_copy(s, n).start()

        @pl.when(jnp.logical_and(s >= LAG, s < 16 + LAG))
        def _():
            sum_far(s - LAG)

        @pl.when(s >= 2 * LAG)
        def _():
            sum_near(s - 2 * LAG)

        @pl.when(s < 16)
        def _():
            sum_cores(s)

        @pl.when(jnp.logical_and(s >= 13, s < 17))
        def _():
            weights(s - 13)

        return carry

    lax.fori_loop(0, 16 + 2 * LAG, step, 0)

    last_i, last_j = wrap(y - zh), wrap(zl * 2 + core - x)
    last = jnp.int32(0)
    for (i, j), s in SLOT.items():
        last = jnp.where(jnp.logical_and(last_i == i, last_j == j), jnp.int32(s), last)
    r_copy(last).wait_recv()
    for h in range(2):
        gout[:, h * (width // 2) : (h + 1) * (width // 2)] = (part[last, h] + zbuf[h]).astype(gout.dtype)
    give = pltpu.make_async_copy(gout, gin_ref, ls.at[3])
    give.start()

    for d in range(2):
        for c in range(3):
            z_copy(d, c).wait_send()
            for i in range(4):
                x_copy(i, d, c).wait_send()
            for q in range(2):
                t_copy(q, d, c).wait_send()
    t_zl().wait_send()
    for q in range(2):
        for e in range(5):
            t_core(q, e).wait_send()

    def drain(s, carry):
        n, own, ahead, _ = place(s)

        @pl.when(jnp.logical_not(own))
        def _():
            d_copy(s, n).wait_send()

        @pl.when(jnp.logical_and(own, ahead != 0))
        def _():
            for h in range(2):
                y_copy(s, n, 0, h).wait_send()

        return carry

    lax.fori_loop(0, 16, drain, 0)
    r_copy(last).wait_send()
    for r in range(4):
        out_copy(r).wait()
    give.wait()


def body(inputs, weight, grad_out):
    tokens, width = inputs.shape
    units = weight.shape[1]
    f32, bf16 = jnp.float32, jnp.bfloat16
    dma = pltpu.SemaphoreType.DMA
    return pl.pallas_call(
        kernel,
        out_shape=(
            jax.ShapeDtypeStruct((tokens, width), bf16),
            jax.ShapeDtypeStruct((width, units), bf16),
        ),
        in_specs=[pl.BlockSpec(memory_space=pl.ANY)] * 3,
        out_specs=[pl.BlockSpec(memory_space=pl.ANY)] * 2,
        scratch_shapes=[
            pltpu.VMEM((16 * tokens, units), bf16),
            pltpu.VMEM((16, width, tokens), bf16),
            pltpu.VMEM((width, units), bf16),
            pltpu.VMEM((width, units), f32),
            pltpu.VMEM((16, 2, tokens, width // 2), f32),
            pltpu.VMEM((8, 2, tokens, width // 2), f32),
            pltpu.VMEM((8, 2, 2, tokens, width // 2), f32),
            pltpu.VMEM((2, tokens, width // 2), f32),
            pltpu.VMEM((width, units), bf16),
            pltpu.VMEM((tokens, width), bf16),
            pltpu.VMEM((tokens, width), bf16),
            dma((2, 3)), dma((2, 3)),
            dma((4, 2, 3)), dma((4, 2, 3)),
            dma((2, 2, 3)), dma((2, 2, 3)),
            dma, dma,
            dma((2, 5)), dma((2, 5)),
            dma((8,)), dma((8,)),
            dma((8, 2)), dma((8, 2, 2)),
            dma, dma,
            dma((4,)), dma((4,)),
        ],
        compiler_params=pltpu.CompilerParams(
            collective_id=0, has_side_effects=True, vmem_limit_bytes=58 * 2**20
        ),
        cost_estimate=pl.CostEstimate(
            flops=4 * 16 * tokens * width * units, bytes_accessed=2 * 2 * width * units, transcendentals=0
        ),
        name="feed_forward_backward",
    )(inputs, weight, grad_out)


def solution(mesh):
    return jax.shard_map(
        body,
        mesh=mesh,
        in_specs=(P("col", "row"), P("row", "col"), P("row", "col")),
        out_specs=(P("col", "row"), P("row", "col")),
        check_vma=False,
    )
```

```python
import jax
import jax.numpy as jnp
from jax import lax
from jax.experimental import pallas as pl
from jax.experimental.pallas import tpu as pltpu
from jax.sharding import PartitionSpec as P

MESH = pl.DeviceIdType.MESH
PIECES = 4

SLOTS = [
    (0, 0), (0, 1), (0, 3), (0, 2), (1, 0), (3, 0), (1, 1), (1, 3),
    (3, 1), (3, 3), (2, 0), (1, 2), (2, 1), (2, 3), (3, 2), (2, 2),
]
SLOT = {ij: s for s, ij in enumerate(SLOTS)}
EVEN = [s for s, (_, j) in enumerate(SLOTS) if j % 2 == 0]
ODD = [s for s, (_, j) in enumerate(SLOTS) if j % 2 == 1]
RANK = [EVEN.index(s) if s in EVEN else ODD.index(s) for s in range(16)]

ORDER = [
    ("tf", 0, 0), ("tc", 0, 0), ("tf", 0, 1), ("fx", 0, 0), ("P", 0), ("fx", 0, 1), ("xa3",), ("xa1",), ("P", 1),
    ("tl",), ("C", 1), ("P", 2), ("xb3",), ("zf", 1), ("P", 4), ("xb1",), ("fx", 3, 0), ("zf", 0), ("tr",),
    ("tc", 0, 1), ("tg", 0, 1), ("C", 4), ("P", 5), ("P", 3), ("C", 5), ("P", 9), ("fx", 1, 1), ("tf", 1, 0),
    ("tf", 1, 1), ("g", 1), ("C", 3), ("P", 8), ("g", 0), ("P", 6), ("C", 9), ("xa2",), ("P", 7), ("tc", 1, 0),
    ("C", 6), ("C", 8), ("tg", 1, 1), ("C", 7), ("P", 10), ("C", 10), ("C", 0), ("tg", 0, 0), ("xb2",),
    ("tg", 1, 0), ("F", 3), ("F", 9), ("F", 4), ("P", 11), ("P", 12), ("C", 11), ("fx", 2, 0), ("F", 5), ("F", 10),
    ("tc", 1, 1), ("C", 12), ("fx", 2, 1), ("F", 8), ("P", 14), ("G", 0, 0), ("F", 1), ("G", 0, 1), ("P", 13),
    ("N", 5), ("N", 3), ("C", 2), ("N", 9), ("C", 14), ("F", 11), ("F", 12), ("P", 15), ("N", 4), ("G", 0, 2),
    ("C", 15), ("F", 2), ("G", 0, 3), ("G", 1, 0), ("F", 15), ("G", 1, 1), ("N", 8), ("N", 10), ("N", 12), ("F", 0),
    ("C", 13), ("F", 7), ("F", 13), ("N", 11), ("N", 1), ("F", 14), ("G", 1, 2), ("G", 1, 3), ("F", 6), ("G", 2, 0),
    ("N", 15), ("N", 7), ("N", 2), ("G", 2, 1), ("N", 6), ("G", 2, 2), ("N", 0), ("N", 14), ("G", 2, 3),
    ("G", 3, 0), ("G", 3, 1), ("N", 13), ("G", 3, 2), ("G", 3, 3),
]


def table(index, values):
    out = jnp.int32(values[0])
    for at, value in enumerate(values[1:], 1):
        if value != values[0]:
            out = jnp.where(index == at, jnp.int32(value), out)
    return out


def kernel(
    in_ref, w_ref, go_ref, gin_ref, gw_ref,
    go, tin, w, acc, part, dbuf, ybuf, zbuf, stage, raw, gout,
    zs, zr, xs, xr, tys, tyr, tzs, tzr, tcs, tcr, ds, dr, ys, yr, rs, rr, ls, os,
):
    row, col = lax.axis_index("row"), lax.axis_index("col")
    zh, x = row // 4, lax.rem(row, 4)
    y, zl, core = col // 4, lax.rem(col // 2, 2), lax.rem(col, 2)
    tokens = raw.shape[0]
    half = tokens // 2
    width = tin.shape[1]
    piece = width // PIECES

    def wrap(v):
        return lax.rem(v + 4, 4)

    def x_peer(d):
        return (zh * 4 + wrap(x + d), col)

    def z_peer(d):
        return (wrap(zh + d) * 4 + x, col)

    def kcol(yy, q, c):
        return (wrap(yy) * 2 + lax.rem(zl + q, 2)) * 2 + c

    def y_peer(d):
        return (row, kcol(y + d, 0, core))

    zl_peer = (row, kcol(y, 1, core))
    core_peer = (row, kcol(y, 0, 1 - core))

    def remote(src, dst, send, recv, to):
        return pltpu.make_async_remote_copy(
            src_ref=src, dst_ref=dst, send_sem=send, recv_sem=recv, device_id=to, device_id_type=MESH
        )

    def rows_of(slot, h):
        return pl.ds(slot * tokens + h * half, half)

    def z_copy(d, c):
        sign, back = 1 - 2 * d, 3 - 2 * d
        h = d if c in (0, 2) else 1 - d
        src, dst = {2: ((back, 0), (2, 0)), 3: ((0, 2), (back, 2))}.get(c, ((0, 0), (back, 0)))
        return remote(
            go.at[rows_of(SLOT[src], h)], go.at[rows_of(SLOT[dst], h)], zs.at[d, c], zr.at[d, c], z_peer(sign)
        )

    def x_copy(i, d, c):
        sign, back = 1 - 2 * d, 3 - 2 * d
        h = d if c != 1 else 1 - d
        src, dst = ((i, back), (i, 2)) if c == 2 else ((i, 0), (i, back))
        return remote(
            go.at[rows_of(SLOT[src], h)], go.at[rows_of(SLOT[dst], h)], xs.at[i, d, c], xr.at[i, d, c], x_peer(sign)
        )

    def t_copy(q, d, c):
        sign = 1 - 2 * d
        h = d if c != 1 else 1 - d
        k = kcol(y - sign, q, core) if c == 2 else kcol(y, q, core)
        block = tin.at[k, pl.ds(h * (width // 2), width // 2)]
        return remote(block, block, tys.at[q, d, c], tyr.at[q, d, c], y_peer(sign))

    def t_zl():
        block = tin.at[kcol(y, 0, core)]
        return remote(block, block, tzs, tzr, zl_peer)

    def t_core(q, e):
        if e < 3:
            block = tin.at[kcol(y + (0, 1, 3)[e], q, core)]
        else:
            block = tin.at[kcol(y + 2, q, core), pl.ds((e - 3) * (width // 2), width // 2)]
        return remote(block, block, tcs.at[q, e], tcr.at[q, e], core_peer)

    def place(s):
        if isinstance(s, int):
            (i, j), rank = SLOTS[s], RANK[s]
        else:
            i, j, rank = table(s, [i for i, _ in SLOTS]), table(s, [j for _, j in SLOTS]), table(s, RANK)
        own = core == lax.rem(x + j, 2)
        return rank, own, lax.rem(zh + i - y + 8, 4), wrap(x + j) // 2

    def d_copy(s, n):
        return remote(part.at[s], dbuf.at[n], ds.at[n], dr.at[n], core_peer)

    def y_copy(s, n, d, p):
        return remote(part.at[s, p], ybuf.at[n, d, p], ys.at[n, p], yr.at[n, d, p], y_peer(1 - 2 * d))

    def r_copy(s, p):
        return remote(part.at[s, p], zbuf.at[p], rs.at[p], rr.at[p], zl_peer)

    loads = [
        pltpu.make_async_copy(go_ref, go.at[pl.ds(0, tokens)], ls.at[0]),
        pltpu.make_async_copy(in_ref, raw, ls.at[1]),
        pltpu.make_async_copy(w_ref, w, ls.at[2]),
    ]
    for load in loads:
        load.start()

    barrier = pltpu.get_barrier_semaphore()
    for to in (x_peer(1), x_peer(3), z_peer(1), z_peer(3), y_peer(1), y_peer(3), zl_peer, core_peer):
        pl.semaphore_signal(barrier, inc=1, device_id=to, device_id_type=MESH)
    pl.semaphore_wait(barrier, 8)

    loads[0].wait()
    for c in range(2):
        for d in range(2):
            z_copy(d, c).start()
            x_copy(0, d, c).start()
    loads[1].wait()
    tin[kcol(y, 0, core)] = raw[...].T
    for c in range(2):
        for d in range(2):
            t_copy(0, d, c).start()
    t_core(0, 0).start()
    acc[...] = jnp.zeros_like(acc)
    loads[2].wait()

    arrivals = {"x": x_copy, "z": z_copy, "t": t_copy, "tl": t_zl, "tc": t_core}
    met = set()
    sent = [("z", d, c) for d in range(2) for c in range(2)]
    sent += [("x", 0, d, c) for d in range(2) for c in range(2)]
    sent += [("t", 0, d, c) for d in range(2) for c in range(2)] + [("tc", 0, 0)]

    def need(*names):
        for name in names:
            if name not in met:
                met.add(name)
                arrivals[name[0]](*name[1:]).wait_recv()

    def begin(*names):
        for name in names:
            sent.append(name)
            arrivals[name[0]](*name[1:]).start()

    def need_block(s):
        i, j = SLOTS[s]
        if j == 0:
            need(*{0: [], 1: [("z", 1, 0), ("z", 1, 1)], 3: [("z", 0, 0), ("z", 0, 1)], 2: [("z", 0, 2), ("z", 1, 2)]}[i])
        elif j != 2:
            need(("x", i, (j == 1) * 1, 0), ("x", i, (j == 1) * 1, 1))
        else:
            for d in range(2):
                passed = ("fx", i, d) in ORDER
                need(("x", i, d, 2) if passed else ("z", 1 - d, 3))

    def sum_cores(s):
        n, own, ahead, _ = place(s)

        @pl.when(own)
        def _():
            d_copy(s, n).wait_recv()

            def add(p, carry):
                part[s, p] += dbuf[n, p]
                return carry

            lax.fori_loop(0, PIECES, add, 0)

            @pl.when(ahead == 2)
            def _():
                for p in range(PIECES // 2):
                    y_copy(s, n, 0, p).start()
                    y_copy(s, n, 1, PIECES // 2 + p).start()

            @pl.when(jnp.logical_or(ahead == 1, ahead == 3))
            def _():
                d = ahead // 2
                for p in range(PIECES // 2):
                    y_copy(s, n, d, (1 - d) * (PIECES // 2) + p).start()

    def sum_far(s):
        n, own, ahead, _ = place(s)

        @pl.when(jnp.logical_and(own, jnp.logical_or(ahead == 1, ahead == 3)))
        def _():
            d = ahead // 2

            def add(e, carry):
                p = d * (PIECES // 2) + e
                y_copy(s, n, d, p).wait_recv()
                part[s, p] += ybuf[n, d, p]
                y_copy(s, n, d, p).start()
                return carry

            lax.fori_loop(0, PIECES // 2, add, 0)

    def sum_near(s):
        n, own, ahead, z_to = place(s)

        @pl.when(jnp.logical_and(own, ahead == 0))
        def _():
            def add(e, carry):
                p = e // 2 + lax.rem(e, 2) * (PIECES // 2)
                for d in range(2):
                    y_copy(s, n, d, p).wait_recv()
                part[s, p] += ybuf[n, 0, p] + ybuf[n, 1, p]

                @pl.when(z_to != zl)
                def _():
                    r_copy(s, p).start()

                return carry

            lax.fori_loop(0, PIECES, add, 0)

    def light(kind, *at):
        if kind == "fx":
            need(("x", *at, 0))
            begin(("x", *at, 2))
        elif kind == "zf":
            need(("z", *at, 0))
            begin(("z", *at, 2))
        elif kind in ("xa1", "xb1", "xa3", "xb3", "xa2", "xb2"):
            i = int(kind[2])
            later = kind[1] == "b"
            need({1: ("z", 1, later * 1), 3: ("z", 0, later * 1), 2: ("z", later * 1, 2)}[i])
            upper = later == (i != 1)
            begin(("x", i, 0, upper * 1), ("x", i, 1, 1 - upper))
        elif kind == "g":
            need(("x", 0, 1 - at[0], 2))
            begin(("z", at[0], 3))
        elif kind == "tl":
            begin(("tl",))
        elif kind == "tr":
            need(("tl",))
            begin(*[("t", 1, d, c) for c in range(2) for d in range(2)], ("tc", 1, 0))
        elif kind == "tf":
            need(("t", *at, 0))
            begin(("t", *at, 2))
        elif kind == "tc":
            need(("t", *at, 0), ("t", *at, 1))
            begin(("tc", at[0], 2 - at[1]))
        elif kind == "tg":
            need(("t", *at, 2))
            begin(("tc", at[0], 3 + at[1]))
        else:
            {"C": sum_cores, "F": sum_far, "N": sum_near}[kind](*at)

    def share(s):
        block = go[pl.ds(pl.multiple_of(s * tokens, tokens), tokens), :]
        for h in range(2):
            both = lax.dot_general(
                block, w[pl.ds(h * (width // 2), width // 2), :], (((1,), (1,)), ((), ())),
                preferred_element_type=jnp.float32,
            )
            for e in range(PIECES // 2):
                part[s, h * (PIECES // 2) + e] = both[:, e * piece : (e + 1) * piece]
        n, own, _, _ = place(s)

        @pl.when(jnp.logical_not(own))
        def _():
            d_copy(s, n).start()

    tile = width // 4

    def out_copy(r):
        at = pl.ds(pl.multiple_of(r * tile, tile), tile)
        return pltpu.make_async_copy(stage.at[at], gw_ref.at[at], os.at[r])

    def weights(g, r):
        ks = []
        for e in range(4):
            i, j = (table(g, [SLOTS[4 * gg + e][axis] for gg in range(4)]) for axis in range(2))
            ks.append(wrap(zh + i) * 4 + wrap(x + j))
        at = pl.ds(pl.multiple_of(r * tile, tile), tile)
        left = jnp.concatenate([tin[k, at, :] for k in ks], axis=1)
        right = go[pl.ds(pl.multiple_of(g * 4 * tokens, 4 * tokens), 4 * tokens), :]
        acc[at, :] += lax.dot_general(left, right, (((1,), (0,)), ((), ())), preferred_element_type=jnp.float32)

        @pl.when(g == 3)
        def _():
            stage[at, :] = acc[at, :].astype(stage.dtype)
            out_copy(r).start()

    heavy = [t for t in ORDER if t[0] in "PG"]
    before, waiting = [], []
    for t in ORDER:
        if t[0] in "PG":
            before.append(waiting)
            waiting = []
        else:
            waiting.append(t)

    def step(h, carry):
        for at, tasks in enumerate(before):

            @pl.when(h == at)
            def _():
                for t in tasks:
                    light(*t)
                if heavy[at][0] == "P":
                    need_block(heavy[at][1])
                else:
                    need(*[("t", q, d, c) for q in range(2) for d in range(2) for c in range(3)], ("tl",))
                    need(*[("tc", q, e) for q in range(2) for e in range(5)])
                    for s in range(4 * heavy[at][1], 4 * heavy[at][1] + 4):
                        need_block(s)

        is_share = table(h, [t[0] == "P" for t in heavy]) == 1

        @pl.when(is_share)
        def _():
            share(table(h, [t[1] if t[0] == "P" else 0 for t in heavy]))

        @pl.when(jnp.logical_not(is_share))
        def _():
            weights(
                table(h, [t[1] if t[0] == "G" else 0 for t in heavy]),
                table(h, [t[2] if t[0] == "G" else 0 for t in heavy]),
            )

        return carry

    lax.fori_loop(0, len(heavy), step, 0)
    for t in waiting:
        light(*t)

    last_i, last_j = wrap(y - zh), wrap(zl * 2 + core - x)
    last = jnp.int32(0)
    for (i, j), s in SLOT.items():
        last = jnp.where(jnp.logical_and(last_i == i, last_j == j), jnp.int32(s), last)
    for e in range(PIECES):
        p = e // 2 + (e % 2) * (PIECES // 2)
        r_copy(last, p).wait_recv()
        gout[:, p * piece : (p + 1) * piece] = (part[last, p] + zbuf[p]).astype(gout.dtype)
    give = pltpu.make_async_copy(gout, gin_ref, ls.at[3])
    give.start()

    for name in sent:
        arrivals[name[0]](*name[1:]).wait_send()

    def drain(s, carry):
        n, own, ahead, _ = place(s)

        @pl.when(jnp.logical_not(own))
        def _():
            d_copy(s, n).wait_send()

        @pl.when(jnp.logical_and(own, ahead != 0))
        def _():
            for p in range(PIECES):
                y_copy(s, n, 0, p).wait_send()

        return carry

    lax.fori_loop(0, 16, drain, 0)
    for p in range(PIECES):
        r_copy(last, p).wait_send()
    for r in range(4):
        out_copy(r).wait()
    give.wait()


def body(inputs, weight, grad_out):
    tokens, width = inputs.shape
    units = weight.shape[1]
    f32, bf16 = jnp.float32, jnp.bfloat16
    dma = pltpu.SemaphoreType.DMA
    blocks = (PIECES, tokens, width // PIECES)
    return pl.pallas_call(
        kernel,
        out_shape=(
            jax.ShapeDtypeStruct((tokens, width), bf16),
            jax.ShapeDtypeStruct((width, units), bf16),
        ),
        in_specs=[pl.BlockSpec(memory_space=pl.ANY)] * 3,
        out_specs=[pl.BlockSpec(memory_space=pl.ANY)] * 2,
        scratch_shapes=[
            pltpu.VMEM((16 * tokens, units), bf16),
            pltpu.VMEM((16, width, tokens), bf16),
            pltpu.VMEM((width, units), bf16),
            pltpu.VMEM((width, units), f32),
            pltpu.VMEM((16, *blocks), f32),
            pltpu.VMEM((8, *blocks), f32),
            pltpu.VMEM((8, 2, *blocks), f32),
            pltpu.VMEM(blocks, f32),
            pltpu.VMEM((width, units), bf16),
            pltpu.VMEM((tokens, width), bf16),
            pltpu.VMEM((tokens, width), bf16),
            dma((2, 4)), dma((2, 4)),
            dma((4, 2, 3)), dma((4, 2, 3)),
            dma((2, 2, 3)), dma((2, 2, 3)),
            dma, dma,
            dma((2, 5)), dma((2, 5)),
            dma((8,)), dma((8,)),
            dma((8, PIECES)), dma((8, 2, PIECES)),
            dma((PIECES,)), dma((PIECES,)),
            dma((4,)), dma((4,)),
        ],
        compiler_params=pltpu.CompilerParams(
            collective_id=0, has_side_effects=True, vmem_limit_bytes=58 * 2**20
        ),
        cost_estimate=pl.CostEstimate(
            flops=4 * 16 * tokens * width * units, bytes_accessed=2 * 2 * width * units, transcendentals=0
        ),
        name="feed_forward_backward",
    )(inputs, weight, grad_out)


def solution(mesh):
    return jax.shard_map(
        body,
        mesh=mesh,
        in_specs=(P("col", "row"), P("row", "col"), P("row", "col")),
        out_specs=(P("col", "row"), P("row", "col")),
        check_vma=False,
    )
```

```python
import jax
import jax.numpy as jnp
from jax import lax
from jax.experimental import pallas as pl
from jax.experimental.pallas import tpu as pltpu
from jax.sharding import PartitionSpec as P

MESH = pl.DeviceIdType.MESH
PIECES = 4
SPANS = 8

SLOTS = [
    (0, 0), (0, 1), (0, 3), (0, 2), (1, 0), (3, 0), (1, 1), (1, 3),
    (3, 1), (3, 3), (2, 0), (1, 2), (2, 1), (2, 3), (3, 2), (2, 2),
]
SLOT = {ij: s for s, ij in enumerate(SLOTS)}
EVEN = [s for s, (_, j) in enumerate(SLOTS) if j % 2 == 0]
ODD = [s for s, (_, j) in enumerate(SLOTS) if j % 2 == 1]
RANK = [EVEN.index(s) if s in EVEN else ODD.index(s) for s in range(16)]

ORDER = [
    ("to",), ("xo",), ("tf", 0, 1), ("P", 0), ("fx", 0, 0), ("fx", 0, 1), ("zo",), ("xa1",), ("C", 0), ("xa3",),
    ("tf", 0, 0), ("P", 3), ("C", 3), ("P", 2), ("tl",), ("P", 5), ("xb1",), ("xb3",), ("C", 5), ("zf", 1),
    ("zf", 0), ("P", 4), ("C", 4), ("tr",), ("P", 6), ("F", 5), ("P", 7), ("tf", 1, 0), ("tg", 0, 0), ("fx", 3, 0),
    ("C", 6), ("tf", 1, 1), ("P", 9), ("g", 0), ("xb2",), ("P", 10), ("C", 9), ("F", 0), ("xa2",), ("g", 1),
    ("C", 10), ("C", 7), ("C", 2), ("P", 1), ("P", 8), ("C", 8), ("tc", 1, 0), ("fx", 1, 1), ("F", 6), ("F", 7),
    ("F", 9), ("C", 1), ("tg", 0, 1), ("tc", 1, 1), ("F", 10), ("tc", 0, 1), ("P", 12), ("C", 12), ("F", 3),
    ("fx", 2, 0), ("P", 13), ("F", 2), ("tc", 0, 0), ("tg", 1, 0), ("fx", 2, 1), ("C", 13), ("tg", 1, 1), ("P", 14),
    ("P", 11), ("N", 6), ("F", 12), ("N", 10), ("N", 9), ("G", 0, 0), ("F", 8), ("G", 0, 1), ("F", 4), ("G", 0, 2),
    ("N", 7), ("C", 11), ("F", 13), ("C", 14), ("P", 15), ("F", 1), ("N", 5), ("N", 8), ("N", 3), ("G", 0, 3),
    ("N", 0), ("G", 1, 0), ("N", 2), ("N", 12), ("C", 15), ("G", 1, 1), ("G", 1, 2), ("N", 4), ("F", 15), ("N", 13),
    ("F", 14), ("F", 11), ("G", 1, 3), ("G", 2, 0), ("N", 1), ("N", 14), ("G", 2, 1), ("N", 11), ("G", 2, 2),
    ("G", 2, 3), ("N", 15), ("G", 3, 0), ("G", 3, 1), ("G", 3, 2), ("G", 3, 3),
]


def table(index, values):
    out = jnp.int32(values[0])
    for at, value in enumerate(values[1:], 1):
        if value != values[0]:
            out = jnp.where(index == at, jnp.int32(value), out)
    return out


def kernel(
    in_ref, w_ref, go_ref, gin_ref, gw_ref,
    go, tin, w, acc, part, dbuf, ybuf, zbuf, stage, raw, gout,
    zs, zr, xs, xr, tys, tyr, tzs, tzr, tcs, tcr, ds, dr, ys, yr, rs, rr, ls, os,
):
    row, col = lax.axis_index("row"), lax.axis_index("col")
    zh, x = row // 4, lax.rem(row, 4)
    y, zl, core = col // 4, lax.rem(col // 2, 2), lax.rem(col, 2)
    tokens = raw.shape[0]
    half = tokens // 2
    width = tin.shape[1]
    piece = width // PIECES

    def wrap(v):
        return lax.rem(v + 4, 4)

    def x_peer(d):
        return (zh * 4 + wrap(x + d), col)

    def z_peer(d):
        return (wrap(zh + d) * 4 + x, col)

    def kcol(yy, q, c):
        return (wrap(yy) * 2 + lax.rem(zl + q, 2)) * 2 + c

    def y_peer(d):
        return (row, kcol(y + d, 0, core))

    zl_peer = (row, kcol(y, 1, core))
    core_peer = (row, kcol(y, 0, 1 - core))

    def remote(src, dst, send, recv, to):
        return pltpu.make_async_remote_copy(
            src_ref=src, dst_ref=dst, send_sem=send, recv_sem=recv, device_id=to, device_id_type=MESH
        )

    def rows_of(slot, h):
        return pl.ds(slot * tokens + h * half, half)

    def z_copy(d, c):
        sign, back = 1 - 2 * d, 3 - 2 * d
        h = d if c in (0, 2) else 1 - d
        src, dst = {2: ((back, 0), (2, 0)), 3: ((0, 2), (back, 2))}.get(c, ((0, 0), (back, 0)))
        return remote(
            go.at[rows_of(SLOT[src], h)], go.at[rows_of(SLOT[dst], h)], zs.at[d, c], zr.at[d, c], z_peer(sign)
        )

    def x_copy(i, d, c):
        sign, back = 1 - 2 * d, 3 - 2 * d
        h = d if c != 1 else 1 - d
        src, dst = ((i, back), (i, 2)) if c == 2 else ((i, 0), (i, back))
        return remote(
            go.at[rows_of(SLOT[src], h)], go.at[rows_of(SLOT[dst], h)], xs.at[i, d, c], xr.at[i, d, c], x_peer(sign)
        )

    def t_copy(q, d, c):
        sign = 1 - 2 * d
        h = d if c != 1 else 1 - d
        k = kcol(y - sign, q, core) if c == 2 else kcol(y, q, core)
        block = tin.at[k, pl.ds(h * (width // 2), width // 2)]
        return remote(block, block, tys.at[q, d, c], tyr.at[q, d, c], y_peer(sign))

    def t_zl():
        block = tin.at[kcol(y, 0, core)]
        return remote(block, block, tzs, tzr, zl_peer)

    def t_core(q, e):
        if e < 3:
            block = tin.at[kcol(y + (0, 1, 3)[e], q, core)]
        else:
            block = tin.at[kcol(y + 2, q, core), pl.ds((e - 3) * (width // 2), width // 2)]
        return remote(block, block, tcs.at[q, e], tcr.at[q, e], core_peer)

    def place(s):
        if isinstance(s, int):
            (i, j), rank = SLOTS[s], RANK[s]
        else:
            i, j, rank = table(s, [i for i, _ in SLOTS]), table(s, [j for _, j in SLOTS]), table(s, RANK)
        own = core == lax.rem(x + j, 2)
        return rank, own, lax.rem(zh + i - y + 8, 4), wrap(x + j) // 2

    halves = PIECES // 2

    def d_copy(s, n, h):
        at = pl.ds(h * halves, halves)
        return remote(part.at[s, at], dbuf.at[n, at], ds.at[n, h], dr.at[n, h], core_peer)

    def y_copy(s, n, d, p):
        return remote(part.at[s, p], ybuf.at[n, d, p], ys.at[n, p], yr.at[n, d, p], y_peer(1 - 2 * d))

    def r_copy(s, p):
        return remote(part.at[s, p], zbuf.at[p], rs.at[p], rr.at[p], zl_peer)

    loads = [
        pltpu.make_async_copy(go_ref, go.at[pl.ds(0, tokens)], ls.at[0]),
        pltpu.make_async_copy(in_ref, raw, ls.at[1]),
        pltpu.make_async_copy(w_ref, w, ls.at[2]),
    ]
    for load in loads:
        load.start()

    barrier = pltpu.get_barrier_semaphore()
    for to in (x_peer(1), x_peer(3), z_peer(1), z_peer(3), y_peer(1), y_peer(3), zl_peer, core_peer):
        pl.semaphore_signal(barrier, inc=1, device_id=to, device_id_type=MESH)
    pl.semaphore_wait(barrier, 8)

    loads[0].wait()
    for d in range(2):
        z_copy(d, 0).start()
        x_copy(0, d, 0).start()
    loads[1].wait()
    tin[kcol(y, 0, core)] = raw[...].T
    for d in range(2):
        t_copy(0, d, 0).start()
    t_core(0, 0).start()
    acc[...] = jnp.zeros_like(acc)
    loads[2].wait()

    arrivals = {"x": x_copy, "z": z_copy, "t": t_copy, "tl": t_zl, "tc": t_core}
    met = set()
    sent = [name for d in range(2) for name in (("z", d, 0), ("x", 0, d, 0), ("t", 0, d, 0))] + [("tc", 0, 0)]

    def need(*names):
        for name in names:
            if name not in met:
                met.add(name)
                arrivals[name[0]](*name[1:]).wait_recv()

    def begin(*names):
        for name in names:
            sent.append(name)
            arrivals[name[0]](*name[1:]).start()

    def need_block(s):
        i, j = SLOTS[s]
        if j == 0:
            need(*{0: [], 1: [("z", 1, 0), ("z", 1, 1)], 3: [("z", 0, 0), ("z", 0, 1)], 2: [("z", 0, 2), ("z", 1, 2)]}[i])
        elif j != 2:
            need(("x", i, (j == 1) * 1, 0), ("x", i, (j == 1) * 1, 1))
        else:
            for d in range(2):
                passed = ("fx", i, d) in ORDER
                need(("x", i, d, 2) if passed else ("z", 1 - d, 3))

    def sum_cores(s):
        n, own, ahead, _ = place(s)

        @pl.when(own)
        def _():
            for h in range(2):
                d_copy(s, n, h).wait_recv()

                def add(e, carry):
                    p = h * halves + e
                    part[s, p] += dbuf[n, p]
                    return carry

                lax.fori_loop(0, halves, add, 0)

                d = jnp.where(ahead == 2, h, 1 - h)

                @pl.when(jnp.logical_or(ahead == 2, ahead == 3 - 2 * h))
                def _():
                    for e in range(halves):
                        y_copy(s, n, d, h * halves + e).start()

    def sum_far(s):
        n, own, ahead, _ = place(s)

        @pl.when(jnp.logical_and(own, jnp.logical_or(ahead == 1, ahead == 3)))
        def _():
            d = ahead // 2

            def add(e, carry):
                p = d * halves + e
                y_copy(s, n, d, p).wait_recv()
                part[s, p] += ybuf[n, d, p]
                y_copy(s, n, d, p).start()
                return carry

            lax.fori_loop(0, halves, add, 0)

    def sum_near(s):
        n, own, ahead, z_to = place(s)

        @pl.when(jnp.logical_and(own, ahead == 0))
        def _():
            def add(e, carry):
                p = e // 2 + lax.rem(e, 2) * halves
                for d in range(2):
                    y_copy(s, n, d, p).wait_recv()
                part[s, p] += ybuf[n, 0, p] + ybuf[n, 1, p]

                @pl.when(z_to != zl)
                def _():
                    r_copy(s, p).start()

                return carry

            lax.fori_loop(0, PIECES, add, 0)

    def light(kind, *at):
        if kind == "zo":
            begin(("z", 0, 1), ("z", 1, 1))
        elif kind == "xo":
            begin(("x", 0, 0, 1), ("x", 0, 1, 1))
        elif kind == "to":
            begin(("t", 0, 0, 1), ("t", 0, 1, 1))
        elif kind == "fx":
            need(("x", *at, 0))
            begin(("x", *at, 2))
        elif kind == "zf":
            need(("z", *at, 0))
            begin(("z", *at, 2))
        elif kind in ("xa1", "xb1", "xa3", "xb3", "xa2", "xb2"):
            i = int(kind[2])
            later = kind[1] == "b"
            need({1: ("z", 1, later * 1), 3: ("z", 0, later * 1), 2: ("z", later * 1, 2)}[i])
            upper = later == (i != 1)
            begin(("x", i, 0, upper * 1), ("x", i, 1, 1 - upper))
        elif kind == "g":
            need(("x", 0, 1 - at[0], 2))
            begin(("z", at[0], 3))
        elif kind == "tl":
            begin(("tl",))
        elif kind == "tr":
            need(("tl",))
            begin(*[("t", 1, d, c) for c in range(2) for d in range(2)], ("tc", 1, 0))
        elif kind == "tf":
            need(("t", *at, 0))
            begin(("t", *at, 2))
        elif kind == "tc":
            need(("t", *at, 0), ("t", *at, 1))
            begin(("tc", at[0], 2 - at[1]))
        elif kind == "tg":
            need(("t", *at, 2))
            begin(("tc", at[0], 3 + at[1]))
        else:
            {"C": sum_cores, "F": sum_far, "N": sum_near}[kind](*at)

    def share(s):
        block = go[pl.ds(pl.multiple_of(s * tokens, tokens), tokens), :]
        n, own, _, _ = place(s)
        for h in range(2):
            both = lax.dot_general(
                block, w[pl.ds(h * (width // 2), width // 2), :], (((1,), (1,)), ((), ())),
                preferred_element_type=jnp.float32,
            )
            for e in range(halves):
                part[s, h * halves + e] = both[:, e * piece : (e + 1) * piece]

            @pl.when(jnp.logical_not(own))
            def _():
                d_copy(s, n, h).start()

    tile = width // 4

    def out_copy(r):
        at = pl.ds(pl.multiple_of(r * tile, tile), tile)
        return pltpu.make_async_copy(stage.at[at], gw_ref.at[at], os.at[r])

    def weights(g, r):
        ks = []
        for e in range(4):
            i, j = (table(g, [SLOTS[4 * gg + e][axis] for gg in range(4)]) for axis in range(2))
            ks.append(wrap(zh + i) * 4 + wrap(x + j))
        at = pl.ds(pl.multiple_of(r * tile, tile), tile)
        left = jnp.concatenate([tin[k, at, :] for k in ks], axis=1)
        right = go[pl.ds(pl.multiple_of(g * 4 * tokens, 4 * tokens), 4 * tokens), :]
        acc[at, :] += lax.dot_general(left, right, (((1,), (0,)), ((), ())), preferred_element_type=jnp.float32)

        @pl.when(g == 3)
        def _():
            stage[at, :] = acc[at, :].astype(stage.dtype)
            out_copy(r).start()

    heavy = [t for t in ORDER if t[0] in "PG"]
    before, waiting = [], []
    for t in ORDER:
        if t[0] in "PG":
            before.append(waiting)
            waiting = []
        else:
            waiting.append(t)

    def step(h, carry):
        for at, tasks in enumerate(before):

            @pl.when(h == at)
            def _():
                for t in tasks:
                    light(*t)
                if heavy[at][0] == "P":
                    need_block(heavy[at][1])
                else:
                    need(*[("t", q, d, c) for q in range(2) for d in range(2) for c in range(3)], ("tl",))
                    need(*[("tc", q, e) for q in range(2) for e in range(5)])
                    for s in range(4 * heavy[at][1], 4 * heavy[at][1] + 4):
                        need_block(s)

        is_share = table(h, [t[0] == "P" for t in heavy]) == 1

        @pl.when(is_share)
        def _():
            share(table(h, [t[1] if t[0] == "P" else 0 for t in heavy]))

        @pl.when(jnp.logical_not(is_share))
        def _():
            weights(
                table(h, [t[1] if t[0] == "G" else 0 for t in heavy]),
                table(h, [t[2] if t[0] == "G" else 0 for t in heavy]),
            )

        return carry

    lax.fori_loop(0, len(heavy), step, 0)
    for t in waiting:
        light(*t)

    last_i, last_j = wrap(y - zh), wrap(zl * 2 + core - x)
    last = jnp.int32(0)
    for (i, j), s in SLOT.items():
        last = jnp.where(jnp.logical_and(last_i == i, last_j == j), jnp.int32(s), last)
    for e in range(PIECES):
        p = e // 2 + (e % 2) * halves
        r_copy(last, p).wait_recv()
        gout[:, p * piece : (p + 1) * piece] = (part[last, p] + zbuf[p]).astype(gout.dtype)
    give = pltpu.make_async_copy(gout, gin_ref, ls.at[3])
    give.start()

    for name in sent:
        arrivals[name[0]](*name[1:]).wait_send()

    def drain(s, carry):
        n, own, ahead, _ = place(s)

        @pl.when(jnp.logical_not(own))
        def _():
            for h in range(2):
                d_copy(s, n, h).wait_send()

        @pl.when(jnp.logical_and(own, ahead != 0))
        def _():
            for p in range(PIECES):
                y_copy(s, n, 0, p).wait_send()

        return carry

    lax.fori_loop(0, 16, drain, 0)
    for p in range(PIECES):
        r_copy(last, p).wait_send()
    for r in range(4):
        out_copy(r).wait()
    give.wait()


def hand_out(gin_held, gw_held, gin_ref, gw_ref, gin, gw, into, out):
    rows = gw.shape[0] // SPANS
    spans = [pl.ds(e * rows, rows) for e in range(SPANS)]
    moves = [(gin_held, gin, gin_ref)] + [(gw_held.at[at], gw.at[at], gw_ref.at[at]) for at in spans]
    reads = [pltpu.make_async_copy(a, b, into.at[e]) for e, (a, b, _) in enumerate(moves)]
    writes = [pltpu.make_async_copy(b, c, out.at[e]) for e, (_, b, c) in enumerate(moves)]
    for read in reads:
        read.start()
    for read, write in zip(reads, writes):
        read.wait()
        write.start()
    for write in writes:
        write.wait()


def body(inputs, weight, grad_out):
    tokens, width = inputs.shape
    units = weight.shape[1]
    f32, bf16 = jnp.float32, jnp.bfloat16
    dma = pltpu.SemaphoreType.DMA
    blocks = (PIECES, tokens, width // PIECES)
    held = pl.pallas_call(
        kernel,
        out_shape=(
            jax.ShapeDtypeStruct((tokens, width), bf16),
            jax.ShapeDtypeStruct((width, units), bf16),
        ),
        in_specs=[pl.BlockSpec(memory_space=pl.ANY)] * 3,
        out_specs=[pl.BlockSpec(memory_space=pl.ANY)] * 2,
        scratch_shapes=[
            pltpu.VMEM((16 * tokens, units), bf16),
            pltpu.VMEM((16, width, tokens), bf16),
            pltpu.VMEM((width, units), bf16),
            pltpu.VMEM((width, units), f32),
            pltpu.VMEM((16, *blocks), f32),
            pltpu.VMEM((8, *blocks), f32),
            pltpu.VMEM((8, 2, *blocks), f32),
            pltpu.VMEM(blocks, f32),
            pltpu.VMEM((width, units), bf16),
            pltpu.VMEM((tokens, width), bf16),
            pltpu.VMEM((tokens, width), bf16),
            dma((2, 4)), dma((2, 4)),
            dma((4, 2, 3)), dma((4, 2, 3)),
            dma((2, 2, 3)), dma((2, 2, 3)),
            dma, dma,
            dma((2, 5)), dma((2, 5)),
            dma((8, 2)), dma((8, 2)),
            dma((8, PIECES)), dma((8, 2, PIECES)),
            dma((PIECES,)), dma((PIECES,)),
            dma((4,)), dma((4,)),
        ],
        compiler_params=pltpu.CompilerParams(
            collective_id=0, has_side_effects=True, vmem_limit_bytes=58 * 2**20
        ),
        cost_estimate=pl.CostEstimate(
            flops=4 * 16 * tokens * width * units, bytes_accessed=2 * 2 * width * units, transcendentals=0
        ),
        name="feed_forward_backward",
    )(inputs, weight, grad_out)
    return pl.pallas_call(
        hand_out,
        out_shape=(
            jax.ShapeDtypeStruct((tokens, width), bf16),
            jax.ShapeDtypeStruct((width, units), bf16),
        ),
        in_specs=[pl.BlockSpec(memory_space=pl.ANY)] * 2,
        out_specs=[pl.BlockSpec(memory_space=pl.ANY)] * 2,
        scratch_shapes=[
            pltpu.VMEM((tokens, width), bf16),
            pltpu.VMEM((width, units), bf16),
            dma((SPANS + 1,)), dma((SPANS + 1,)),
        ],
        compiler_params=pltpu.CompilerParams(vmem_limit_bytes=58 * 2**20),
        name="hand_out",
    )(*held)


def solution(mesh):
    return jax.shard_map(
        body,
        mesh=mesh,
        in_specs=(P("col", "row"), P("row", "col"), P("row", "col")),
        out_specs=(P("col", "row"), P("row", "col")),
        check_vma=False,
    )
```

```python
import jax
import jax.numpy as jnp
from jax import lax
from jax.experimental import pallas as pl
from jax.experimental.pallas import tpu as pltpu
from jax.sharding import PartitionSpec as P

MESH = pl.DeviceIdType.MESH
PIECES = 4
SPANS = 4

SLOTS = [
    (0, 0), (0, 1), (0, 3), (0, 2), (1, 0), (3, 0), (1, 1), (1, 3),
    (3, 1), (3, 3), (2, 0), (1, 2), (2, 1), (2, 3), (3, 2), (2, 2),
]
SLOT = {ij: s for s, ij in enumerate(SLOTS)}
EVEN = [s for s, (_, j) in enumerate(SLOTS) if j % 2 == 0]
ODD = [s for s, (_, j) in enumerate(SLOTS) if j % 2 == 1]
RANK = [EVEN.index(s) if s in EVEN else ODD.index(s) for s in range(16)]

ORDER = [
    ("to",), ("xo",), ("tf", 0, 1), ("P", 0), ("fx", 0, 0), ("fx", 0, 1), ("zo",), ("xa1",), ("C", 0), ("xa3",),
    ("tf", 0, 0), ("P", 3), ("C", 3), ("P", 2), ("tl",), ("P", 5), ("xb1",), ("xb3",), ("C", 5), ("zf", 1),
    ("P", 4), ("zf", 0), ("C", 4), ("tr",), ("P", 6), ("F", 5), ("P", 7), ("tf", 1, 0), ("tg", 0, 0), ("fx", 3, 0),
    ("C", 6), ("tf", 1, 1), ("P", 9), ("g", 0), ("xb2",), ("P", 10), ("C", 9), ("F", 0), ("xa2",), ("g", 1),
    ("C", 10), ("C", 7), ("C", 2), ("P", 1), ("P", 8), ("C", 8), ("tc", 1, 0), ("fx", 1, 1), ("F", 6), ("F", 7),
    ("F", 9), ("C", 1), ("tg", 0, 1), ("tc", 1, 1), ("F", 10), ("tc", 0, 1), ("P", 12), ("C", 12), ("F", 3),
    ("fx", 2, 0), ("P", 13), ("F", 2), ("tc", 0, 0), ("tg", 1, 0), ("fx", 2, 1), ("C", 13), ("tg", 1, 1), ("P", 14),
    ("P", 11), ("N", 6), ("F", 12), ("N", 10), ("N", 9), ("G", 0, 0), ("F", 8), ("G", 0, 1), ("F", 4), ("G", 0, 2),
    ("N", 7), ("C", 11), ("F", 13), ("C", 14), ("P", 15), ("F", 1), ("N", 5), ("N", 8), ("N", 3), ("G", 0, 3),
    ("N", 0), ("G", 1, 0), ("N", 2), ("N", 12), ("C", 15), ("G", 1, 1), ("G", 1, 2), ("N", 4), ("F", 15), ("N", 13),
    ("F", 14), ("F", 11), ("G", 1, 3), ("G", 2, 0), ("N", 1), ("N", 14), ("G", 2, 1), ("N", 11), ("G", 2, 2),
    ("G", 2, 3), ("N", 15), ("G", 3, 0), ("G", 3, 1), ("G", 3, 2), ("G", 3, 3),
]


def table(index, values):
    out = jnp.int32(values[0])
    for at, value in enumerate(values[1:], 1):
        if value != values[0]:
            out = jnp.where(index == at, jnp.int32(value), out)
    return out


def kernel(
    in_ref, w_ref, go_ref, gin_ref, gw_ref,
    go, tin, w, acc, part, dbuf, ybuf, zbuf, stage, raw, gout,
    zs, zr, xs, xr, tys, tyr, tzs, tzr, tcs, tcr, ds, dr, ys, yr, rs, rr, ls, os,
):
    row, col = lax.axis_index("row"), lax.axis_index("col")
    zh, x = row // 4, lax.rem(row, 4)
    y, zl, core = col // 4, lax.rem(col // 2, 2), lax.rem(col, 2)
    tokens = raw.shape[0]
    half = tokens // 2
    width = tin.shape[1]
    piece = width // PIECES

    def wrap(v):
        return lax.rem(v + 4, 4)

    def x_peer(d):
        return (zh * 4 + wrap(x + d), col)

    def z_peer(d):
        return (wrap(zh + d) * 4 + x, col)

    def kcol(yy, q, c):
        return (wrap(yy) * 2 + lax.rem(zl + q, 2)) * 2 + c

    def y_peer(d):
        return (row, kcol(y + d, 0, core))

    zl_peer = (row, kcol(y, 1, core))
    core_peer = (row, kcol(y, 0, 1 - core))

    def remote(src, dst, send, recv, to):
        return pltpu.make_async_remote_copy(
            src_ref=src, dst_ref=dst, send_sem=send, recv_sem=recv, device_id=to, device_id_type=MESH
        )

    def rows_of(slot, h):
        return pl.ds(slot * tokens + h * half, half)

    def z_copy(d, c):
        sign, back = 1 - 2 * d, 3 - 2 * d
        h = d if c in (0, 2) else 1 - d
        src, dst = {2: ((back, 0), (2, 0)), 3: ((0, 2), (back, 2))}.get(c, ((0, 0), (back, 0)))
        return remote(
            go.at[rows_of(SLOT[src], h)], go.at[rows_of(SLOT[dst], h)], zs.at[d, c], zr.at[d, c], z_peer(sign)
        )

    def x_copy(i, d, c):
        sign, back = 1 - 2 * d, 3 - 2 * d
        h = d if c != 1 else 1 - d
        src, dst = ((i, back), (i, 2)) if c == 2 else ((i, 0), (i, back))
        return remote(
            go.at[rows_of(SLOT[src], h)], go.at[rows_of(SLOT[dst], h)], xs.at[i, d, c], xr.at[i, d, c], x_peer(sign)
        )

    def t_copy(q, d, c):
        sign = 1 - 2 * d
        h = d if c != 1 else 1 - d
        k = kcol(y - sign, q, core) if c == 2 else kcol(y, q, core)
        block = tin.at[k, pl.ds(h * (width // 2), width // 2)]
        return remote(block, block, tys.at[q, d, c], tyr.at[q, d, c], y_peer(sign))

    def t_zl():
        block = tin.at[kcol(y, 0, core)]
        return remote(block, block, tzs, tzr, zl_peer)

    def t_core(q, e):
        if e < 3:
            block = tin.at[kcol(y + (0, 1, 3)[e], q, core)]
        else:
            block = tin.at[kcol(y + 2, q, core), pl.ds((e - 3) * (width // 2), width // 2)]
        return remote(block, block, tcs.at[q, e], tcr.at[q, e], core_peer)

    def place(s):
        if isinstance(s, int):
            (i, j), rank = SLOTS[s], RANK[s]
        else:
            i, j, rank = table(s, [i for i, _ in SLOTS]), table(s, [j for _, j in SLOTS]), table(s, RANK)
        own = core == lax.rem(x + j, 2)
        return rank, own, lax.rem(zh + i - y + 8, 4), wrap(x + j) // 2

    halves = PIECES // 2

    def d_copy(s, n, h):
        at = pl.ds(h * halves, halves)
        return remote(part.at[s, at], dbuf.at[n, at], ds.at[n, h], dr.at[n, h], core_peer)

    def y_copy(s, n, d, p):
        return remote(part.at[s, p], ybuf.at[n, d, p], ys.at[n, p], yr.at[n, d, p], y_peer(1 - 2 * d))

    def r_copy(s, p):
        return remote(part.at[s, p], zbuf.at[p], rs.at[p], rr.at[p], zl_peer)

    loads = [
        pltpu.make_async_copy(go_ref, go.at[pl.ds(0, tokens)], ls.at[0]),
        pltpu.make_async_copy(in_ref, raw, ls.at[1]),
        pltpu.make_async_copy(w_ref, w, ls.at[2]),
    ]
    for load in loads:
        load.start()

    barrier = pltpu.get_barrier_semaphore()
    for to in (x_peer(1), x_peer(3), z_peer(1), z_peer(3), y_peer(1), y_peer(3), zl_peer, core_peer):
        pl.semaphore_signal(barrier, inc=1, device_id=to, device_id_type=MESH)
    pl.semaphore_wait(barrier, 8)

    loads[0].wait()
    for d in range(2):
        z_copy(d, 0).start()
        x_copy(0, d, 0).start()
    loads[1].wait()
    tin[kcol(y, 0, core)] = raw[...].T
    for d in range(2):
        t_copy(0, d, 0).start()
    t_core(0, 0).start()
    acc[...] = jnp.zeros_like(acc)
    loads[2].wait()

    arrivals = {"x": x_copy, "z": z_copy, "t": t_copy, "tl": t_zl, "tc": t_core}
    met = set()
    sent = [name for d in range(2) for name in (("z", d, 0), ("x", 0, d, 0), ("t", 0, d, 0))] + [("tc", 0, 0)]

    def need(*names):
        for name in names:
            if name not in met:
                met.add(name)
                arrivals[name[0]](*name[1:]).wait_recv()

    def begin(*names):
        for name in names:
            sent.append(name)
            arrivals[name[0]](*name[1:]).start()

    def need_block(s):
        i, j = SLOTS[s]
        if j == 0:
            need(*{0: [], 1: [("z", 1, 0), ("z", 1, 1)], 3: [("z", 0, 0), ("z", 0, 1)], 2: [("z", 0, 2), ("z", 1, 2)]}[i])
        elif j != 2:
            need(("x", i, (j == 1) * 1, 0), ("x", i, (j == 1) * 1, 1))
        else:
            for d in range(2):
                passed = ("fx", i, d) in ORDER
                need(("x", i, d, 2) if passed else ("z", 1 - d, 3))

    def sum_cores(s):
        n, own, ahead, _ = place(s)

        @pl.when(own)
        def _():
            for h in range(2):
                d_copy(s, n, h).wait_recv()

                def add(e, carry):
                    p = h * halves + e
                    part[s, p] += dbuf[n, p]
                    return carry

                lax.fori_loop(0, halves, add, 0)

                d = jnp.where(ahead == 2, h, 1 - h)

                @pl.when(jnp.logical_or(ahead == 2, ahead == 3 - 2 * h))
                def _():
                    for e in range(halves):
                        y_copy(s, n, d, h * halves + e).start()

    def sum_far(s):
        n, own, ahead, _ = place(s)

        @pl.when(jnp.logical_and(own, jnp.logical_or(ahead == 1, ahead == 3)))
        def _():
            d = ahead // 2

            def add(e, carry):
                p = d * halves + e
                y_copy(s, n, d, p).wait_recv()
                part[s, p] += ybuf[n, d, p]
                y_copy(s, n, d, p).start()
                return carry

            lax.fori_loop(0, halves, add, 0)

    def sum_near(s):
        n, own, ahead, z_to = place(s)

        @pl.when(jnp.logical_and(own, ahead == 0))
        def _():
            def add(e, carry):
                p = e // 2 + lax.rem(e, 2) * halves
                for d in range(2):
                    y_copy(s, n, d, p).wait_recv()
                part[s, p] += ybuf[n, 0, p] + ybuf[n, 1, p]

                @pl.when(z_to != zl)
                def _():
                    r_copy(s, p).start()

                return carry

            lax.fori_loop(0, PIECES, add, 0)

    def light(kind, *at):
        if kind == "zo":
            begin(("z", 0, 1), ("z", 1, 1))
        elif kind == "xo":
            begin(("x", 0, 0, 1), ("x", 0, 1, 1))
        elif kind == "to":
            begin(("t", 0, 0, 1), ("t", 0, 1, 1))
        elif kind == "fx":
            need(("x", *at, 0))
            begin(("x", *at, 2))
        elif kind == "zf":
            need(("z", *at, 0))
            begin(("z", *at, 2))
        elif kind in ("xa1", "xb1", "xa3", "xb3", "xa2", "xb2"):
            i = int(kind[2])
            later = kind[1] == "b"
            need({1: ("z", 1, later * 1), 3: ("z", 0, later * 1), 2: ("z", later * 1, 2)}[i])
            upper = later == (i != 1)
            begin(("x", i, 0, upper * 1), ("x", i, 1, 1 - upper))
        elif kind == "g":
            need(("x", 0, 1 - at[0], 2))
            begin(("z", at[0], 3))
        elif kind == "tl":
            begin(("tl",))
        elif kind == "tr":
            need(("tl",))
            begin(*[("t", 1, d, c) for c in range(2) for d in range(2)], ("tc", 1, 0))
        elif kind == "tf":
            need(("t", *at, 0))
            begin(("t", *at, 2))
        elif kind == "tc":
            need(("t", *at, 0), ("t", *at, 1))
            begin(("tc", at[0], 2 - at[1]))
        elif kind == "tg":
            need(("t", *at, 2))
            begin(("tc", at[0], 3 + at[1]))
        else:
            {"C": sum_cores, "F": sum_far, "N": sum_near}[kind](*at)

    def share(s):
        block = go[pl.ds(pl.multiple_of(s * tokens, tokens), tokens), :]
        n, own, _, _ = place(s)
        for h in range(2):
            both = lax.dot_general(
                block, w[pl.ds(h * (width // 2), width // 2), :], (((1,), (1,)), ((), ())),
                preferred_element_type=jnp.float32,
            )
            for e in range(halves):
                part[s, h * halves + e] = both[:, e * piece : (e + 1) * piece]

            @pl.when(jnp.logical_not(own))
            def _():
                d_copy(s, n, h).start()

    tile = width // 4

    def out_copy(r):
        at = pl.ds(pl.multiple_of(r * tile, tile), tile)
        return pltpu.make_async_copy(stage.at[at], gw_ref.at[at], os.at[r])

    def weights(g, r):
        ks = []
        for e in range(4):
            i, j = (table(g, [SLOTS[4 * gg + e][axis] for gg in range(4)]) for axis in range(2))
            ks.append(wrap(zh + i) * 4 + wrap(x + j))
        at = pl.ds(pl.multiple_of(r * tile, tile), tile)
        left = jnp.concatenate([tin[k, at, :] for k in ks], axis=1)
        right = go[pl.ds(pl.multiple_of(g * 4 * tokens, 4 * tokens), 4 * tokens), :]
        acc[at, :] += lax.dot_general(left, right, (((1,), (0,)), ((), ())), preferred_element_type=jnp.float32)

        @pl.when(g == 3)
        def _():
            stage[at, :] = acc[at, :].astype(stage.dtype)
            out_copy(r).start()

    heavy = [t for t in ORDER if t[0] in "PG"]
    before, waiting = [], []
    for t in ORDER:
        if t[0] in "PG":
            before.append(waiting)
            waiting = []
        else:
            waiting.append(t)

    def step(h, carry):
        def prepare(at):
            for t in before[at]:
                light(*t)
            if heavy[at][0] == "P":
                need_block(heavy[at][1])
            else:
                need(*[("t", q, d, c) for q in range(2) for d in range(2) for c in range(3)], ("tl",))
                need(*[("tc", q, e) for q in range(2) for e in range(5)])
                for s in range(4 * heavy[at][1], 4 * heavy[at][1] + 4):
                    need_block(s)

        for group in range(0, len(heavy), 4):

            @pl.when(jnp.logical_and(h >= group, h < group + 4))
            def _():
                for at in range(group, min(group + 4, len(heavy))):
                    pl.when(h == at)(lambda at=at: prepare(at))

        is_share = table(h, [t[0] == "P" for t in heavy]) == 1

        @pl.when(is_share)
        def _():
            share(table(h, [t[1] if t[0] == "P" else 0 for t in heavy]))

        @pl.when(jnp.logical_not(is_share))
        def _():
            weights(
                table(h, [t[1] if t[0] == "G" else 0 for t in heavy]),
                table(h, [t[2] if t[0] == "G" else 0 for t in heavy]),
            )

        return carry

    lax.fori_loop(0, len(heavy), step, 0)
    for t in waiting:
        light(*t)

    last_i, last_j = wrap(y - zh), wrap(zl * 2 + core - x)
    last = jnp.int32(0)
    for (i, j), s in SLOT.items():
        last = jnp.where(jnp.logical_and(last_i == i, last_j == j), jnp.int32(s), last)
    for e in range(PIECES):
        p = e // 2 + (e % 2) * halves
        r_copy(last, p).wait_recv()
        gout[:, p * piece : (p + 1) * piece] = (part[last, p] + zbuf[p]).astype(gout.dtype)
    give = pltpu.make_async_copy(gout, gin_ref, ls.at[3])
    give.start()

    for name in sent:
        arrivals[name[0]](*name[1:]).wait_send()

    def drain(s, carry):
        n, own, ahead, _ = place(s)

        @pl.when(jnp.logical_not(own))
        def _():
            for h in range(2):
                d_copy(s, n, h).wait_send()

        @pl.when(jnp.logical_and(own, ahead != 0))
        def _():
            for p in range(PIECES):
                y_copy(s, n, 0, p).wait_send()

        return carry

    lax.fori_loop(0, 16, drain, 0)
    for p in range(PIECES):
        r_copy(last, p).wait_send()
    for r in range(4):
        out_copy(r).wait()
    give.wait()


def hand_out(gin_held, gw_held, gin_ref, gw_ref, gin, gw, into, out):
    rows = gw.shape[0] // SPANS
    spans = [pl.ds(e * rows, rows) for e in range(SPANS)]
    moves = [(gin_held, gin, gin_ref)] + [(gw_held.at[at], gw.at[at], gw_ref.at[at]) for at in spans]
    reads = [pltpu.make_async_copy(a, b, into.at[e]) for e, (a, b, _) in enumerate(moves)]
    writes = [pltpu.make_async_copy(b, c, out.at[e]) for e, (_, b, c) in enumerate(moves)]
    for read in reads:
        read.start()
    for read, write in zip(reads, writes):
        read.wait()
        write.start()
    for write in writes:
        write.wait()


def body(inputs, weight, grad_out):
    tokens, width = inputs.shape
    units = weight.shape[1]
    f32, bf16 = jnp.float32, jnp.bfloat16
    dma = pltpu.SemaphoreType.DMA
    blocks = (PIECES, tokens, width // PIECES)
    held = pl.pallas_call(
        kernel,
        out_shape=(
            jax.ShapeDtypeStruct((tokens, width), bf16),
            jax.ShapeDtypeStruct((width, units), bf16),
        ),
        in_specs=[pl.BlockSpec(memory_space=pl.ANY)] * 3,
        out_specs=[pl.BlockSpec(memory_space=pl.ANY)] * 2,
        scratch_shapes=[
            pltpu.VMEM((16 * tokens, units), bf16),
            pltpu.VMEM((16, width, tokens), bf16),
            pltpu.VMEM((width, units), bf16),
            pltpu.VMEM((width, units), f32),
            pltpu.VMEM((16, *blocks), f32),
            pltpu.VMEM((8, *blocks), f32),
            pltpu.VMEM((8, 2, *blocks), f32),
            pltpu.VMEM(blocks, f32),
            pltpu.VMEM((width, units), bf16),
            pltpu.VMEM((tokens, width), bf16),
            pltpu.VMEM((tokens, width), bf16),
            dma((2, 4)), dma((2, 4)),
            dma((4, 2, 3)), dma((4, 2, 3)),
            dma((2, 2, 3)), dma((2, 2, 3)),
            dma, dma,
            dma((2, 5)), dma((2, 5)),
            dma((8, 2)), dma((8, 2)),
            dma((8, PIECES)), dma((8, 2, PIECES)),
            dma((PIECES,)), dma((PIECES,)),
            dma((4,)), dma((4,)),
        ],
        compiler_params=pltpu.CompilerParams(
            collective_id=0, has_side_effects=True, vmem_limit_bytes=58 * 2**20
        ),
        cost_estimate=pl.CostEstimate(
            flops=4 * 16 * tokens * width * units, bytes_accessed=2 * 2 * width * units, transcendentals=0
        ),
        name="feed_forward_backward",
    )(inputs, weight, grad_out)
    return pl.pallas_call(
        hand_out,
        out_shape=(
            jax.ShapeDtypeStruct((tokens, width), bf16),
            jax.ShapeDtypeStruct((width, units), bf16),
        ),
        in_specs=[pl.BlockSpec(memory_space=pl.ANY)] * 2,
        out_specs=[pl.BlockSpec(memory_space=pl.ANY)] * 2,
        scratch_shapes=[
            pltpu.VMEM((tokens, width), bf16),
            pltpu.VMEM((width, units), bf16),
            dma((SPANS + 1,)), dma((SPANS + 1,)),
        ],
        compiler_params=pltpu.CompilerParams(vmem_limit_bytes=58 * 2**20),
        name="hand_out",
    )(*held)


def solution(mesh):
    return jax.shard_map(
        body,
        mesh=mesh,
        in_specs=(P("col", "row"), P("row", "col"), P("row", "col")),
        out_specs=(P("col", "row"), P("row", "col")),
        check_vma=False,
    )
```
